32 devices in a mesh: groups: 2 (over y), tile: 4 (over z), tm: 4 (over x, core).
Axes of the slice: x: 2, y: 2, z: 4, core: 2. Of those that a mesh axis runs over, the one named last changes fastest.
Arguments:
- shocks: bfloat16 [32768, 512], P(('groups', 'tile'), 'tm'), parts along dimension 0, may hold values from -6 to 6
- volatility: float32 [16384], P('tile'), may hold values from 0.3 to 3
Outputs:
- covariance: float32 [8, 4, 1024, 16384], P('groups', 'tm', None, 'tile'), parts along dimension 0
The draws below stay inside these ranges and needn't reach their ends.
There are 2 independent parts, one for each index of `groups`. The reference program is written for one: setup_inputs(seed, part) draws one part's arguments, and reference() takes and returns one part's arrays. A program takes and returns all parts, laid end to end along the dimension named above; an argument that names none is the same for every part. Nothing has to cross between parts.
All inputs are finite; a program needn't handle non-finite values.
Results may differ from the reference program's by a relative error of at most 0.023.
Values may be sent and summed in bfloat16 or wider, within the bound.
A program may use at most 192 MiB of HBM per device.

```python
import math
import jax
import jax.numpy as jnp
from jax import lax

ASSETS = 16384
LAGS = 64
PERIODS = 512
PIECE = 1024
N_TILE = 4
N_TM = 4


def draw_shocks(key, part):
    key = jax.random.fold_in(key, 11)
    key_white, key_own, key_common, key_load = jax.random.split(key, 4)
    white_part = jax.random.normal(key_white, (ASSETS, PERIODS), jnp.float32)
    own_part = jax.random.normal(key_own, (ASSETS, PERIODS + 1), jnp.float32)
    common_part = jax.random.normal(key_common, (PERIODS + 1,), jnp.float32)
    own_weight = 0.6
    common_weight = 0.8
    loading = jax.random.uniform(key_load, (ASSETS, 1), jnp.float32, 0.5, 1.5)
    levels = own_weight * own_part + common_weight * loading * common_part[None, :]
    change = levels[:, 1:] - levels[:, :-1]
    return jnp.clip(white_part + 1.2 * change, -6.0, 6.0).astype(jnp.bfloat16)


def steps_of(key, dims, shards, smallest, top_value):
    level = 1.0
    for axis_at, parts in shards:
        steps = jax.random.uniform(jax.random.fold_in(jax.random.fold_in(key, 6), axis_at), (parts,), jnp.float32, smallest / len(shards), top_value / len(shards))
        level = level * jnp.repeat(jnp.exp(steps), dims[axis_at] // parts).reshape((-1,) + (1,) * (len(dims) - 1 - axis_at))
    return level


def setup_inputs(seed: int = 0, part: int = 0) -> dict:
    key_of = jax.random.split(jax.random.key(seed), 3)
    own_keys = jax.random.split(jax.random.fold_in(key_of[2], part), 3)
    return {
        "shocks": draw_shocks(jax.random.fold_in(jax.random.fold_in(key_of[2], part), 71), part),
        "volatility": jnp.clip(jnp.exp(math.log(3.0) - 2.3025851 * jax.random.uniform(key_of[1], (ASSETS,), jnp.float32) ** steps_of(key_of[1], (ASSETS,), ((0, 4),), -0.2, 0.2)), 0.3, 3.0),
    }


def reference(shocks, volatility):
    scaled = (shocks.astype(jnp.float32) * volatility[:, None]).astype(jnp.bfloat16)
    series = scaled.astype(jnp.float32)
    smooth = 0.5 * series
    padded = jnp.pad(series, ((0, 0), (LAGS, 0)))
    for lag_step in range(1, LAGS + 1):
        weight = 1.0 - lag_step / (LAGS + 1.0)
        smooth = smooth + weight * padded[:, LAGS - lag_step:LAGS - lag_step + PERIODS]
    filtered = smooth.astype(jnp.bfloat16).astype(jnp.float32)
    half_sum = jnp.dot(series, filtered.T, precision=lax.Precision.HIGHEST)
    long_run = (half_sum + half_sum.T) / PERIODS
    return long_run.reshape(N_TILE, N_TM, PIECE, ASSETS)
```

```python
import jax
import jax.numpy as jnp
from jax import lax
from jax.experimental import pallas as pl
from jax.experimental.pallas import tpu as pltpu
from jax.sharding import PartitionSpec as P

LAGS = 64


def swap(value, axis, mask):
    count = lax.axis_size(axis)
    return lax.ppermute(value, axis, [(source, source ^ mask) for source in range(count)])


def pass_on(value, axis):
    count = lax.axis_size(axis)
    return lax.ppermute(value, axis, [(source, (source + 1) % count) for source in range(count)])


def block_kernel(part_count, block_ref, *refs):
    parts, weighted_ref, out_ref = refs[:part_count], refs[part_count], refs[-1]
    rows = jnp.concatenate([part[...] for part in parts], axis=1)
    out_ref[0, 0] = jnp.dot(rows, weighted_ref[...], preferred_element_type=jnp.float32)


def write_block(block, parts, weighted, whole, block_count):
    piece_rows, slab_len = parts[0].shape
    period_count, column_count = weighted.shape
    row_step = min(piece_rows, 256)
    column_step = min(column_count, 2048)
    part_spec = pl.BlockSpec((row_step, slab_len), lambda c, r, b: (r, 0))
    in_specs = [part_spec] * len(parts)
    in_specs.append(pl.BlockSpec((period_count, column_step), lambda c, r, b: (0, c)))
    operands = [block, *parts, weighted]
    aliases = {}
    if whole is not None:
        in_specs.append(pl.BlockSpec(memory_space=pl.ANY))
        aliases = {len(operands): 0}
        operands.append(whole)
    return pl.pallas_call(
        lambda *refs: block_kernel(len(parts), *refs),
        out_shape=jax.ShapeDtypeStruct((block_count, 1, piece_rows, column_count), jnp.float32),
        grid_spec=pltpu.PrefetchScalarGridSpec(
            num_scalar_prefetch=1,
            grid=(column_count // column_step, piece_rows // row_step),
            in_specs=in_specs,
            out_specs=pl.BlockSpec(
                (1, 1, row_step, column_step), lambda c, r, b: (b[0], 0, r, c)
            ),
        ),
        input_output_aliases=aliases,
        compiler_params=pltpu.CompilerParams(vmem_limit_bytes=32 * 2**20),
        cost_estimate=pl.CostEstimate(
            flops=2 * piece_rows * period_count * column_count,
            bytes_accessed=4 * piece_rows * column_count + 2 * period_count * column_count,
            transcendentals=0,
        ),
    )(*operands)


def local(shocks, volatility):
    scaled = (shocks.astype(jnp.float32) * volatility[:, None]).astype(jnp.bfloat16)
    row_count, slab_len = scaled.shape
    slab_parts = lax.axis_size("tm")
    tile_parts = lax.axis_size("tile")
    slab_index = lax.axis_index("tm")
    tile_index = lax.axis_index("tile")
    piece_rows = row_count // slab_parts
    period_count = slab_parts * slab_len

    parts = []
    for mask in range(slab_parts):
        other = (slab_index ^ mask) * piece_rows
        rows = lax.dynamic_slice_in_dim(scaled, other, piece_rows, 0)
        parts.append(swap(rows, "tm", mask) if mask else rows)

    arrived = [parts]
    for _ in range(tile_parts - 1):
        arrived.append([pass_on(part, "tile") for part in arrived[-1]])

    pieces = jnp.stack(parts)[None]
    mask = slab_parts // 2
    masks = [0]
    while mask:
        pieces = jnp.concatenate([pieces, swap(pieces, "tm", mask)], axis=0)
        masks = masks + [m ^ mask for m in masks]
        mask //= 2
    ordered = jnp.stack([
        jnp.concatenate([pieces[at, m ^ q] for m in range(slab_parts)], axis=1)
        for at, q in sorted(enumerate(masks), key=lambda pair: pair[1])
    ])
    series = jnp.concatenate(
        [
            lax.dynamic_index_in_dim(ordered, slab_index ^ p, 0, keepdims=False)
            for p in range(slab_parts)
        ],
        axis=0,
    )

    place = jnp.arange(period_count, dtype=jnp.int32)
    time = ((place // slab_len) ^ slab_index) * slab_len + place % slab_len
    band = jnp.maximum(0, LAGS + 1 - jnp.abs(time[:, None] - time[None, :])).astype(jnp.bfloat16)
    weighted = lax.dot_general(
        band, series, (((1,), (1,)), ((), ())), preferred_element_type=jnp.float32
    )
    weighted = (weighted * (1.0 / ((LAGS + 1) * period_count))).astype(jnp.bfloat16)

    whole = None
    for step in range(tile_parts):
        block = lax.rem(tile_index - step + tile_parts, tile_parts).reshape(1)
        whole = write_block(block, arrived[step], weighted, whole, tile_parts)
    return whole


def solution(mesh):
    in_specs = (P(("groups", "tile"), "tm"), P("tile"))
    out_specs = P("groups", "tm", None, "tile")
    return jax.shard_map(local, mesh=mesh, in_specs=in_specs, out_specs=out_specs, check_vma=False)
```

```python
import jax
import jax.numpy as jnp
from jax import lax
from jax.experimental import pallas as pl
from jax.experimental.pallas import tpu as pltpu
from jax.sharding import PartitionSpec as P

LAGS = 64
VMEM = 48 * 2**20
ANY = pl.BlockSpec(memory_space=pl.ANY)


def pass_on(value, axis):
    count = lax.axis_size(axis)
    return lax.ppermute(value, axis, [(source, (source + 1) % count) for source in range(count)])


def beside(part):
    return jnp.concatenate([part[m] for m in range(part.shape[0])], axis=1)


def exchange(scaled, steps):
    slab_count, piece_rows, slab_len = scaled.shape
    tile_count = lax.axis_size("tile")

    def kernel(scaled_ref, pieces, *refs):
        arrived = refs[:steps]
        own_sem, slab_send, slab_recv, piece_send, piece_recv, ring_send, ring_recv = refs[steps:]
        own = lax.axis_index("tm")
        tile = lax.axis_index("tile")
        right = lax.rem(tile + 1, tile_count)
        left = lax.rem(tile + tile_count - 1, tile_count)

        def remote(source, target, send, recv, device):
            return pltpu.make_async_remote_copy(
                src_ref=source,
                dst_ref=target,
                send_sem=send,
                recv_sem=recv,
                device_id=device,
                device_id_type=pl.DeviceIdType.MESH,
            )

        barrier = pltpu.get_barrier_semaphore()
        others = [{"tm": own ^ m} for m in range(1, slab_count)] + [{"tile": right}, {"tile": left}]
        for other in others:
            pl.semaphore_signal(
                barrier, inc=1, device_id=other, device_id_type=pl.DeviceIdType.MESH
            )
        pl.semaphore_wait(barrier, len(others))

        slabs = {
            m: remote(
                scaled_ref.at[own ^ m],
                pieces.at[0, m],
                slab_send.at[m],
                slab_recv.at[m],
                {"tm": own ^ m},
            )
            for m in range(1, slab_count)
        }

        def ring(step, m):
            if step:
                source = arrived[step - 1].at[m]
            else:
                source = pieces.at[0, m] if m else scaled_ref.at[own]
            return remote(
                source,
                arrived[step].at[m],
                ring_send.at[step, m],
                ring_recv.at[step, m],
                {"tile": right},
            )

        rings = {(step, m): ring(step, m) for step in range(steps) for m in range(slab_count)}
        local = pltpu.make_async_copy(scaled_ref.at[own], pieces.at[0, 0], own_sem)
        for m in reversed(range(1, slab_count)):
            slabs[m].start()
        rings[0, 0].start()
        local.start()
        for m in range(1, slab_count):
            slabs[m].wait_recv()
            rings[0, m].start()
        local.wait()

        held, sent = [0], []
        mask = slab_count // 2
        first = True
        while mask:
            moves = [
                remote(
                    pieces.at[q],
                    pieces.at[q ^ mask],
                    piece_send.at[q ^ mask],
                    piece_recv.at[q ^ mask],
                    {"tm": own ^ mask},
                )
                for q in held
            ]
            for move in moves:
                move.start()
            if first:
                first = False
                for step in range(1, steps):
                    for m in range(slab_count):
                        rings[step - 1, m].wait_recv()
                        rings[step, m].start()
            for move in moves:
                move.wait_recv()
            sent += moves
            held = held + [q ^ mask for q in held]
            mask //= 2
        for m in range(slab_count):
            rings[steps - 1, m].wait_recv()
        for move in [*slabs.values(), *rings.values(), *sent]:
            move.wait_send()

    piece = jax.ShapeDtypeStruct((slab_count, piece_rows, slab_len), jnp.bfloat16)
    everything = jax.ShapeDtypeStruct((slab_count, *piece.shape), jnp.bfloat16)
    dma = pltpu.SemaphoreType.DMA
    return pl.pallas_call(
        kernel,
        out_shape=[everything] + [piece] * steps,
        in_specs=[ANY],
        out_specs=[ANY] * (1 + steps),
        scratch_shapes=[dma(())]
        + [dma((slab_count,))] * 4
        + [dma((steps, slab_count))] * 2,
        compiler_params=pltpu.CompilerParams(collective_id=0, has_side_effects=True),
    )(scaled)


def weigh(pieces, slab_index):
    piece_count, slab_count, piece_rows, slab_len = pieces.shape
    period_count = slab_count * slab_len
    scale = 1.0 / ((LAGS + 1) * period_count)

    def band(own, partner):
        row = lax.broadcasted_iota(jnp.int32, (slab_len, slab_len), 0)
        column = lax.broadcasted_iota(jnp.int32, (slab_len, slab_len), 1)
        distance = row - column
        rows = []
        for u in range(slab_count):
            blocks = []
            for v in range(slab_count):
                apart = ((own ^ u) - (partner ^ v)) * slab_len
                weight = jnp.maximum(0, LAGS + 1 - jnp.abs(distance + apart))
                blocks.append(weight.astype(jnp.float32).astype(jnp.bfloat16))
            rows.append(jnp.concatenate(blocks, axis=1))
        return jnp.concatenate(rows, axis=0)

    def kernel(index_ref, pieces_ref, out_ref):
        own = index_ref[0]
        for q in range(piece_count):
            partner = own ^ q
            product = lax.dot_general(
                band(own, partner),
                beside(pieces_ref[q]),
                (((1,), (1,)), ((), ())),
                preferred_element_type=jnp.float32,
            )
            out_ref[partner] = (product * scale).astype(jnp.bfloat16)

    return pl.pallas_call(
        kernel,
        out_shape=jax.ShapeDtypeStruct((piece_count, period_count, piece_rows), jnp.bfloat16),
        in_specs=[pl.BlockSpec(memory_space=pltpu.SMEM)]
        + [pl.BlockSpec(memory_space=pltpu.VMEM)],
        out_specs=pl.BlockSpec(memory_space=pltpu.VMEM),
        compiler_params=pltpu.CompilerParams(vmem_limit_bytes=VMEM),
        cost_estimate=pl.CostEstimate(
            flops=piece_count * piece_rows * period_count,
            bytes_accessed=piece_rows * period_count,
            transcendentals=0,
        ),
    )(slab_index.reshape(1), pieces)


def write_block(block, piece, weighted, whole, block_count, width=1024):
    slab_count, piece_rows, slab_len = piece.shape[1:]
    chunk_count, period_count, chunk_columns = weighted.shape
    column_step = min(chunk_columns, width)
    split = chunk_columns // column_step

    def kernel(block_ref, piece_ref, weighted_ref, *refs):
        refs[-1][0, 0] = jnp.dot(
            beside(piece_ref[0]), weighted_ref[0], preferred_element_type=jnp.float32
        )

    in_specs = [
        pl.BlockSpec((1, slab_count, piece_rows, slab_len), lambda c, b: (0, 0, 0, 0)),
        pl.BlockSpec(
            (1, period_count, column_step),
            lambda c, b: (lax.div(c, split), 0, lax.rem(c, split)),
        ),
    ]
    operands = [block, piece, weighted]
    aliases = {}
    if whole is not None:
        aliases = {len(operands): 0}
        operands.append(whole)
        in_specs.append(ANY)
    return pl.pallas_call(
        kernel,
        out_shape=jax.ShapeDtypeStruct(
            (block_count, 1, piece_rows, chunk_count * chunk_columns), jnp.float32
        ),
        grid_spec=pltpu.PrefetchScalarGridSpec(
            num_scalar_prefetch=1,
            grid=(chunk_count * split,),
            in_specs=in_specs,
            out_specs=pl.BlockSpec(
                (1, 1, piece_rows, column_step), lambda c, b: (b[0], 0, 0, c)
            ),
        ),
        input_output_aliases=aliases,
        compiler_params=pltpu.CompilerParams(vmem_limit_bytes=VMEM),
        cost_estimate=pl.CostEstimate(
            flops=2 * piece_rows * period_count * chunk_count * chunk_columns,
            bytes_accessed=4 * piece_rows * chunk_count * chunk_columns,
            transcendentals=0,
        ),
    )(*operands)


def local(shocks, volatility):
    scaled = (shocks.astype(jnp.float32) * volatility[:, None]).astype(jnp.bfloat16)
    row_count, slab_len = scaled.shape
    slab_parts = lax.axis_size("tm")
    tile_parts = lax.axis_size("tile")
    slab_index = lax.axis_index("tm")
    tile_index = lax.axis_index("tile")
    piece_rows = row_count // slab_parts

    steps = min(2, tile_parts - 1)
    pieces, *arrived = exchange(scaled.reshape(slab_parts, piece_rows, slab_len), steps)
    while len(arrived) < tile_parts - 1:
        arrived.append(pass_on(arrived[-1], "tile"))
    weighted = weigh(pieces, slab_index)
    if piece_rows % 128:
        weighted = weighted.transpose(1, 0, 2).reshape(1, -1, row_count)
    whole = None
    for step in range(tile_parts):
        block = lax.rem(tile_index - step + tile_parts, tile_parts).reshape(1)
        piece = arrived[step - 1][None] if step else pieces
        whole = write_block(block, piece, weighted, whole, tile_parts)
    return whole


def solution(mesh):
    in_specs = (P(("groups", "tile"), "tm"), P("tile"))
    out_specs = P("groups", "tm", None, "tile")
    return jax.shard_map(local, mesh=mesh, in_specs=in_specs, out_specs=out_specs, check_vma=False)
```

```python
import jax
import jax.numpy as jnp
from jax import lax
from jax.experimental import pallas as pl
from jax.experimental.pallas import tpu as pltpu
from jax.sharding import PartitionSpec as P

LAGS = 64
VMEM = 48 * 2**20
ANY = pl.BlockSpec(memory_space=pl.ANY)


def pass_on(value, axis):
    count = lax.axis_size(axis)
    return lax.ppermute(value, axis, [(source, (source + 1) % count) for source in range(count)])


def beside(part):
    return jnp.concatenate([part[m] for m in range(part.shape[0])], axis=1)


def exchange(scaled, steps):
    slab_count, piece_rows, slab_len = scaled.shape
    tile_count = lax.axis_size("tile")
    counts = [slab_count] * (steps - 1) + [slab_count - 1]

    def kernel(scaled_ref, pieces, *refs):
        arrived = refs[:steps]
        own_sem, slab_send, slab_recv, piece_send, piece_recv, ring_send, ring_recv = refs[steps:]
        own = lax.axis_index("tm")
        tile = lax.axis_index("tile")
        right = lax.rem(tile + 1, tile_count)
        left = lax.rem(tile + tile_count - 1, tile_count)

        def remote(source, target, send, recv, device):
            return pltpu.make_async_remote_copy(
                src_ref=source,
                dst_ref=target,
                send_sem=send,
                recv_sem=recv,
                device_id=device,
                device_id_type=pl.DeviceIdType.MESH,
            )

        barrier = pltpu.get_barrier_semaphore()
        others = [{"tm": own ^ m} for m in range(1, slab_count)] + [{"tile": right}, {"tile": left}]
        for other in others:
            pl.semaphore_signal(
                barrier, inc=1, device_id=other, device_id_type=pl.DeviceIdType.MESH
            )
        pl.semaphore_wait(barrier, len(others))

        slabs = {
            m: remote(
                scaled_ref.at[own ^ m],
                pieces.at[0, m],
                slab_send.at[m],
                slab_recv.at[m],
                {"tm": own ^ m},
            )
            for m in range(1, slab_count)
        }

        def ring(step, m):
            if step:
                source = arrived[step - 1].at[m]
            else:
                source = pieces.at[0, m] if m else scaled_ref.at[own]
            return remote(
                source,
                arrived[step].at[m],
                ring_send.at[step, m],
                ring_recv.at[step, m],
                {"tile": right},
            )

        rings = {(step, m): ring(step, m) for step in range(steps) for m in range(counts[step])}
        local = pltpu.make_async_copy(scaled_ref.at[own], pieces.at[0, 0], own_sem)
        for m in reversed(range(1, slab_count)):
            slabs[m].start()
        rings[0, 0].start()
        local.start()
        for m in range(1, slab_count):
            slabs[m].wait_recv()
            rings[0, m].start()
        local.wait()

        held, sent = [0], []
        mask = slab_count // 2
        first = True
        while mask:
            moves = [
                remote(
                    pieces.at[q],
                    pieces.at[q ^ mask],
                    piece_send.at[q ^ mask],
                    piece_recv.at[q ^ mask],
                    {"tm": own ^ mask},
                )
                for q in held
            ]
            for move in moves:
                move.start()
            if first:
                first = False
                for step in range(1, steps):
                    for m in range(counts[step]):
                        rings[step - 1, m].wait_recv()
                        rings[step, m].start()
            for move in moves:
                move.wait_recv()
            sent += moves
            held = held + [q ^ mask for q in held]
            mask //= 2
        for m in range(counts[-2] - 1, counts[-2]):
            rings[steps - 2, m].wait_recv()
        for m in range(counts[-1]):
            rings[steps - 1, m].wait_recv()
        for move in [*slabs.values(), *rings.values(), *sent]:
            move.wait_send()

    piece = jax.ShapeDtypeStruct((slab_count, piece_rows, slab_len), jnp.bfloat16)
    part = jax.ShapeDtypeStruct((slab_count - 1, piece_rows, slab_len), jnp.bfloat16)
    everything = jax.ShapeDtypeStruct((slab_count, *piece.shape), jnp.bfloat16)
    dma = pltpu.SemaphoreType.DMA
    return pl.pallas_call(
        kernel,
        out_shape=[everything] + [piece] * (steps - 1) + [part],
        in_specs=[ANY],
        out_specs=[ANY] * (1 + steps),
        scratch_shapes=[dma(())]
        + [dma((slab_count,))] * 4
        + [dma((steps, slab_count))] * 2,
        compiler_params=pltpu.CompilerParams(collective_id=0, has_side_effects=True),
    )(scaled)


def weigh(pieces, slab_index):
    piece_count, slab_count, piece_rows, slab_len = pieces.shape
    period_count = slab_count * slab_len
    scale = 1.0 / ((LAGS + 1) * period_count)

    def band(own, partner):
        row = lax.broadcasted_iota(jnp.int32, (slab_len, slab_len), 0)
        column = lax.broadcasted_iota(jnp.int32, (slab_len, slab_len), 1)
        distance = row - column
        rows = []
        for u in range(slab_count):
            blocks = []
            for v in range(slab_count):
                apart = ((own ^ u) - (partner ^ v)) * slab_len
                weight = jnp.maximum(0, LAGS + 1 - jnp.abs(distance + apart))
                blocks.append(weight.astype(jnp.float32).astype(jnp.bfloat16))
            rows.append(jnp.concatenate(blocks, axis=1))
        return jnp.concatenate(rows, axis=0)

    def kernel(index_ref, pieces_ref, out_ref):
        own = index_ref[0]
        for q in range(piece_count):
            partner = own ^ q
            product = lax.dot_general(
                band(own, partner),
                beside(pieces_ref[q]),
                (((1,), (1,)), ((), ())),
                preferred_element_type=jnp.float32,
            )
            out_ref[partner] = (product * scale).astype(jnp.bfloat16)

    return pl.pallas_call(
        kernel,
        out_shape=jax.ShapeDtypeStruct((piece_count, period_count, piece_rows), jnp.bfloat16),
        in_specs=[pl.BlockSpec(memory_space=pltpu.SMEM)]
        + [pl.BlockSpec(memory_space=pltpu.VMEM)],
        out_specs=pl.BlockSpec(memory_space=pltpu.VMEM),
        compiler_params=pltpu.CompilerParams(vmem_limit_bytes=VMEM),
        cost_estimate=pl.CostEstimate(
            flops=piece_count * piece_rows * period_count,
            bytes_accessed=piece_rows * period_count,
            transcendentals=0,
        ),
    )(slab_index.reshape(1), pieces)


def write_block(block, parts, weighted, whole, block_count, width=1024):
    piece_rows = parts[0].shape[2]
    chunk_count, period_count, chunk_columns = weighted.shape
    column_step = min(chunk_columns, width)
    split = chunk_columns // column_step

    def kernel(block_ref, *refs):
        left = [beside(ref[0]) for ref in refs[: len(parts)]]
        left = jnp.concatenate(left, axis=1) if len(left) > 1 else left[0]
        refs[-1][0, 0] = jnp.dot(
            left, refs[len(parts)][0], preferred_element_type=jnp.float32
        )

    in_specs = [
        *[pl.BlockSpec((1, *part.shape[1:]), lambda c, b: (0, 0, 0, 0)) for part in parts],
        pl.BlockSpec(
            (1, period_count, column_step),
            lambda c, b: (lax.div(c, split), 0, lax.rem(c, split)),
        ),
    ]
    operands = [block, *parts, weighted]
    aliases = {}
    if whole is not None:
        aliases = {len(operands): 0}
        operands.append(whole)
        in_specs.append(ANY)
    return pl.pallas_call(
        kernel,
        out_shape=jax.ShapeDtypeStruct(
            (block_count, 1, piece_rows, chunk_count * chunk_columns), jnp.float32
        ),
        grid_spec=pltpu.PrefetchScalarGridSpec(
            num_scalar_prefetch=1,
            grid=(chunk_count * split,),
            in_specs=in_specs,
            out_specs=pl.BlockSpec(
                (1, 1, piece_rows, column_step), lambda c, b: (b[0], 0, 0, c)
            ),
        ),
        input_output_aliases=aliases,
        compiler_params=pltpu.CompilerParams(vmem_limit_bytes=VMEM),
        cost_estimate=pl.CostEstimate(
            flops=2 * piece_rows * period_count * chunk_count * chunk_columns,
            bytes_accessed=4 * piece_rows * chunk_count * chunk_columns,
            transcendentals=0,
        ),
    )(*operands)


def local(shocks, volatility):
    scaled = (shocks.astype(jnp.float32) * volatility[:, None]).astype(jnp.bfloat16)
    row_count, slab_len = scaled.shape
    slab_parts = lax.axis_size("tm")
    tile_parts = lax.axis_size("tile")
    slab_index = lax.axis_index("tm")
    tile_index = lax.axis_index("tile")
    piece_rows = row_count // slab_parts

    pieces, near, most = exchange(scaled.reshape(slab_parts, piece_rows, slab_len), 2)
    arrived = [[pieces], [near[None]], [most[None], pass_on(near[-1:], "tile")[None]]]
    while len(arrived) < tile_parts:
        arrived.append([pass_on(part, "tile") for part in arrived[-1]])
    weighted = weigh(pieces, slab_index)
    if piece_rows % 128:
        weighted = weighted.transpose(1, 0, 2).reshape(1, -1, row_count)
    whole = None
    for step in range(tile_parts):
        block = lax.rem(tile_index - step + tile_parts, tile_parts).reshape(1)
        whole = write_block(block, arrived[step], weighted, whole, tile_parts)
    return whole


def solution(mesh):
    in_specs = (P(("groups", "tile"), "tm"), P("tile"))
    out_specs = P("groups", "tm", None, "tile")
    return jax.shard_map(local, mesh=mesh, in_specs=in_specs, out_specs=out_specs, check_vma=False)
```
